32 devices in a mesh: groups: 2 (over y), row: 8 (over z, x), col: 2 (over core).
Axes of the slice: x: 2, y: 2, z: 4, core: 2. Of those that a mesh axis runs over, the one named last changes fastest.
Arguments:
- cot: float32 [24576, 12288], P(('groups', 'row'), 'col'), parts along dimension 0, as said below
- panel_late: bfloat16 [24576, 512], P(('groups', 'row', 'col')), parts along dimension 0, may hold values from -0.0546875 to 0.0546875
- panel_early: bfloat16 [24576, 512], P(('groups', 'row', 'col')), parts along dimension 0, may hold values from -0.0546875 to 0.0546875
- inv_late: float32 [1024, 512], P('groups'), parts along dimension 0, as said below
- inv_early: float32 [1024, 512], P('groups'), parts along dimension 0, as said below
Outputs:
- late_cot: float32 [24576, 512], P(('groups', 'row', 'col')), parts along dimension 0
- early_cot: float32 [24576, 512], P(('groups', 'row', 'col')), parts along dimension 0
- late_diag: float32 [1024, 512], P(('groups', 'row')), parts along dimension 0
- early_diag: float32 [1024, 512], P(('groups', 'row')), parts along dimension 0
The draws below stay inside these ranges and needn't reach their ends.
There are 2 independent parts, one for each index of `groups`. The reference program is written for one: setup_inputs(seed, part) draws one part's arguments, and reference() takes and returns one part's arrays. A program takes and returns all parts, laid end to end along the dimension named above; each array names one. Nothing has to cross between parts.
Inputs may be any that keep to these rules, and one draw needn't show every extreme that they name: cot holds a symmetric matrix C in the column order given in the reference program. inv_late is upper triangular with a diagonal of 1 to 2. inv_early is upper triangular with a diagonal of 1 to 2.
All inputs are finite; a program needn't handle non-finite values.
Results may differ from the reference program's by a relative error of at most 0.0003.
Values may be sent and summed in bfloat16 or wider, within the bound.
No kernel may reach another device: no remote copies, remote signals or barrier semaphores. Data moves between devices by JAX's collectives and lax.ppermute only.
A program may use at most 128 MiB of HBM per device.

```python
import math
import jax
import jax.numpy as jnp
from jax import lax

M = 12288
B = 512
PIECE = 768
N_ROW = 8
N_COL = 2


def draw_cot(key, part):
    base = jax.random.normal(jax.random.fold_in(key, 3), (M, M), jnp.float32)
    symmetric = (base + base.T) * 0.7071
    return symmetric.reshape(M, N_ROW, N_COL, PIECE).transpose(0, 2, 1, 3).reshape(M, M)


def upper_factor(key):
    diagonal = jax.random.uniform(jax.random.fold_in(key, 1), (B,), jnp.float32, 1.0, 2.0)
    offdiag = jax.random.normal(jax.random.fold_in(key, 2), (B, B), jnp.float32) / math.sqrt(B)
    rows_idx = jnp.arange(B, dtype=jnp.int32)[:, None]
    cols_idx = jnp.arange(B, dtype=jnp.int32)[None, :]
    upper_part = jnp.where(cols_idx > rows_idx, offdiag, jnp.float32(0.0))
    on_diag = jnp.where(cols_idx == rows_idx, diagonal[:, None], jnp.float32(0.0))
    return upper_part + on_diag


def draw_inv_late(key, part):
    return upper_factor(jax.random.fold_in(key, 31))


def draw_inv_early(key, part):
    return upper_factor(jax.random.fold_in(key, 47))


def shard_levels(rng, dims, split, smallest, largest):
    loudness = 1.0
    for dim, shards_of in split:
        heights = jax.random.uniform(jax.random.fold_in(jax.random.fold_in(rng, 6), dim), (shards_of,), jnp.float32, smallest / len(split), largest / len(split))
        loudness = loudness * jnp.repeat(jnp.exp(heights), dims[dim] // shards_of).reshape((-1,) + (1,) * (len(dims) - 1 - dim))
    return loudness


def bell_draw(stream_key, dims, scale, most, pieces=(), held_as=jnp.bfloat16):
    loudness = shard_levels(stream_key, dims, pieces, -0.22, 0.18) if pieces else 1.0
    entries = jax.random.normal(stream_key, dims, jnp.float32) * scale * loudness
    return jnp.minimum(jnp.maximum(entries, -most), most).astype(held_as)


def setup_inputs(seed: int = 0, part: int = 0) -> dict:
    seeds = jax.random.split(jax.random.key(seed), 6)
    own_keys = jax.random.split(jax.random.fold_in(seeds[5], part), 6)
    cot = draw_cot(jax.random.fold_in(jax.random.fold_in(seeds[5], part), 71), part)
    panel_late = bell_draw(own_keys[1], (M, B), M ** -0.5, 0.0546875, ((0, 16),))
    panel_early = bell_draw(own_keys[2], (M, B), M ** -0.5, 0.0546875, ((0, 16),))
    inv_late = draw_inv_late(jax.random.fold_in(jax.random.fold_in(seeds[5], part), 71), part)
    inv_early = draw_inv_early(jax.random.fold_in(jax.random.fold_in(seeds[5], part), 71), part)
    return {"cot": cot, "panel_late": panel_late, "panel_early": panel_early, "inv_late": inv_late, "inv_early": inv_early}


def highest(left, right):
    return jnp.dot(left, right, precision=lax.Precision.HIGHEST, preferred_element_type=jnp.float32)


def reference(cot, panel_late, panel_early, inv_late, inv_early):
    natural = cot.reshape(M, N_COL, N_ROW, PIECE).transpose(0, 2, 1, 3).reshape(M, M)
    positions = jnp.arange(M, dtype=jnp.int32)
    trailing = (positions >= B)[:, None]
    late_f = jnp.where(trailing, panel_late.astype(jnp.float32), jnp.float32(0.0))
    early_f = panel_early.astype(jnp.float32)
    late_grad = jnp.where(trailing, highest(natural, late_f), jnp.float32(0.0))
    late_cot = -2.0 * highest(late_grad, inv_late.T)
    late_diag = -highest(late_cot.T, late_f)
    symmetric = 0.5 * (late_diag + late_diag.T)
    cross = highest(late_cot.T, early_f)
    top_block = early_f[:B]
    corner = cross + highest(symmetric, top_block)
    corner_full = jnp.concatenate([corner, jnp.zeros((M - B, B), jnp.float32)], axis=0)
    early_grad = highest(natural, early_f) + highest(late_cot, top_block) + corner_full
    early_cot = -2.0 * highest(early_grad, inv_early.T)
    early_diag = -highest(early_cot.T, early_f)
    return (late_cot, early_cot, late_diag, early_diag)
```

```python
import jax
import jax.numpy as jnp
from jax import lax
from jax.sharding import PartitionSpec as P

SWAP = [(0, 1), (1, 0)]


def highest(left, right):
    return jnp.dot(left, right, precision=lax.Precision.HIGHEST, preferred_element_type=jnp.float32)


def inner_rows(left, right):
    return lax.dot_general(
        left,
        right,
        (((0,), (0,)), ((), ())),
        precision=lax.Precision.HIGHEST,
        preferred_element_type=jnp.float32,
    )


def ring_order(n_rows):
    return list(range(0, n_rows, 2)) + list(range(n_rows - 1, 0, -2))


def flip(n, bit):
    return [(i, i ^ bit) for i in range(n)]


def sum_cols(value, col_id):
    half = value.shape[0] // 2
    low, high = value[:half], value[half:]
    first = col_id == 0
    return jnp.where(first, low, high) + lax.ppermute(jnp.where(first, high, low), "col", SWAP)


def scatter_sum(value, row_id, col_id, n_rows):
    block = value.shape[0] // n_rows
    width = value.shape[1]
    value = value.reshape(n_rows, 2, block // 2, width)
    first = col_id == 0
    kept = jnp.where(first, value[:, 0], value[:, 1])
    sent = jnp.where(first, value[:, 1], value[:, 0])
    value = kept + lax.ppermute(sent, "col", SWAP)
    bit = 1
    while bit < n_rows:
        pairs = value.reshape(-1, 2, block // 2, width)
        zero = (row_id & bit) == 0
        kept = jnp.where(zero, pairs[:, 0], pairs[:, 1])
        sent = jnp.where(zero, pairs[:, 1], pairs[:, 0])
        value = kept + lax.ppermute(sent, "row", flip(n_rows, bit))
        bit *= 2
    return value[0]


def join_cols(value, col_id):
    other = lax.ppermute(value, "col", SWAP)
    first = col_id == 0
    return jnp.concatenate([jnp.where(first, value, other), jnp.where(first, other, value)], axis=0)


def gather_blocks(value, row_id, col_id, n_rows):
    half, width = value.shape
    value = value[None]
    bit = n_rows // 2
    while bit:
        other = lax.ppermute(value, "row", flip(n_rows, bit))
        zero = (row_id & bit) == 0
        value = jnp.stack([jnp.where(zero, value, other), jnp.where(zero, other, value)], axis=1)
        value = value.reshape(-1, half, width)
        bit //= 2
    other = lax.ppermute(value, "col", SWAP)
    first = col_id == 0
    both = jnp.stack([jnp.where(first, value, other), jnp.where(first, other, value)], axis=1)
    return both.reshape(-1, width)


def spread_top(top, row_id, col_id, n_rows):
    half = top.shape[0] // 2
    first = col_id == 0
    low, high = top[:half], top[half:]
    own = jnp.where(first, low, lax.ppermute(high, "col", [(0, 1)]))
    bit = n_rows // 2
    step = n_rows
    while bit:
        sent = lax.ppermute(own, "row", [(i, i + bit) for i in range(0, n_rows, step)])
        own = jnp.where(row_id % step == bit, sent, own)
        step = bit
        bit //= 2
    return join_cols(own, col_id)


def add_piece(total, matrix, piece, start):
    block = lax.dynamic_slice_in_dim(matrix, start, piece.shape[0], 1)
    part = highest(block, piece.astype(jnp.float32))
    return part if total is None else total + part


def ring_product(matrix, piece, n_rows, row_id):
    order = ring_order(n_rows)
    where = [0] * n_rows
    for place, row in enumerate(order):
        where[row] = place
    order_of = jnp.array(order, jnp.int32)
    place = jnp.array(where, jnp.int32)[row_id]
    ahead = [(order[i], order[(i + 1) % n_rows]) for i in range(n_rows)]
    back = [(b, a) for a, b in ahead]
    rows = piece.shape[0]
    half = rows // 2

    def origin(step):
        return order_of[(place + step) % n_rows] * rows

    total = add_piece(None, matrix, piece, row_id * rows)
    from_before, from_after = piece, piece
    for step in range(1, n_rows // 2):
        from_before = lax.ppermute(from_before, "row", ahead)
        from_after = lax.ppermute(from_after, "row", back)
        total = add_piece(total, matrix, from_before, origin(n_rows - step))
        total = add_piece(total, matrix, from_after, origin(step))
    low = lax.ppermute(from_before[:half], "row", ahead)
    high = lax.ppermute(from_after[half:], "row", back)
    far = jnp.concatenate([low, high], axis=0)
    total = add_piece(total, matrix, far, origin(n_rows // 2))
    return total, far


def whole_product(matrix, piece):
    return highest(matrix, lax.all_gather(piece, "row", axis=0, tiled=True).astype(jnp.float32))


def per_device(cot, panel_late, panel_early, inv_late, inv_early):
    strip_rows = cot.shape[0]
    piece_rows = panel_late.shape[0]
    panel_width = panel_late.shape[1]
    n_rows = lax.axis_size("row")
    row_id = lax.axis_index("row")
    col_id = lax.axis_index("col")
    own_start = row_id * strip_rows + col_id * piece_rows
    positions = own_start + jnp.arange(piece_rows, dtype=jnp.int32)
    trailing = (positions >= panel_width)[:, None]
    late_masked = jnp.where(trailing, panel_late, jnp.zeros_like(panel_late))
    ring = n_rows <= 16 and n_rows & (n_rows - 1) == 0 and piece_rows >= panel_width
    if ring:
        top_block = spread_top(panel_early[:panel_width], row_id, col_id, n_rows)
        late_part, far = ring_product(cot, late_masked, n_rows, row_id)
        panel_next, far = lax.optimization_barrier((panel_early, far))
        early_part, _ = ring_product(cot, panel_next, n_rows, row_id)
    else:
        late_part = whole_product(cot, late_masked)
        early_all = lax.all_gather(panel_early, "row", axis=0, tiled=True)
        early_part = highest(cot, early_all.astype(jnp.float32))
        strips = -(-panel_width // strip_rows)
        own_top = early_all[: strips * piece_rows]
        both = lax.all_gather(own_top.reshape(strips, piece_rows, panel_width), "col", axis=1)
        top_block = both.reshape(-1, panel_width)[:panel_width]
    top_block = top_block.astype(jnp.float32)
    late_grad = jnp.where(trailing, sum_cols(late_part, col_id), jnp.float32(0.0))
    late_cot = -2.0 * highest(late_grad, inv_late.T)
    late_f = late_masked.astype(jnp.float32)
    early_f = panel_early.astype(jnp.float32)
    late_term = -inner_rows(late_cot, late_f)
    cross_term = inner_rows(late_cot, early_f)
    corner_term = cross_term + highest(0.5 * (late_term + late_term.T), top_block)
    if ring:
        corner = scatter_sum(corner_term, row_id, col_id, n_rows)
        corner = gather_blocks(corner, row_id, col_id, n_rows)
        late_diag = join_cols(scatter_sum(late_term, row_id, col_id, n_rows), col_id)
    else:
        corner = lax.psum(corner_term, ("row", "col"))
        late_diag = lax.psum(lax.psum_scatter(late_term, "row", scatter_dimension=0, tiled=True), "col")
    corner_padded = jnp.concatenate(
        [corner, jnp.zeros((piece_rows, panel_width), jnp.float32)], axis=0
    )
    corner_rows = lax.dynamic_slice_in_dim(
        corner_padded, jnp.minimum(own_start, panel_width), piece_rows, 0
    )
    extra = highest(late_cot, top_block) + corner_rows
    early_grad = sum_cols(early_part, col_id) + extra
    early_cot = -2.0 * highest(early_grad, inv_early.T)
    early_term = -inner_rows(early_cot, early_f)
    if ring:
        early_diag = join_cols(scatter_sum(early_term, row_id, col_id, n_rows), col_id)
    else:
        early_diag = lax.psum(lax.psum_scatter(early_term, "row", scatter_dimension=0, tiled=True), "col")
    return (late_cot, early_cot, late_diag, early_diag)


def solution(mesh):
    return jax.shard_map(
        per_device,
        mesh=mesh,
        in_specs=(
            P(("groups", "row"), "col"),
            P(("groups", "row", "col"), None),
            P(("groups", "row", "col"), None),
            P("groups", None),
            P("groups", None),
        ),
        out_specs=(
            P(("groups", "row", "col"), None),
            P(("groups", "row", "col"), None),
            P(("groups", "row"), None),
            P(("groups", "row"), None),
        ),
        check_vma=False,
    )
```

```python
import jax
import jax.numpy as jnp
from jax import lax
from jax.experimental import pallas as pl
from jax.experimental.pallas import tpu as pltpu
from jax.sharding import PartitionSpec as P

SWAP = [(0, 1), (1, 0)]


def high(left, right, contract=(1, 0)):
    return lax.dot_general(
        left,
        right,
        (((contract[0],), (contract[1],)), ((), ())),
        precision=lax.Precision.HIGH,
        preferred_element_type=jnp.float32,
    )


def highest(left, right):
    return jnp.dot(left, right, precision=lax.Precision.HIGHEST, preferred_element_type=jnp.float32)


def inner_rows(left, right):
    return lax.dot_general(
        left,
        right,
        (((0,), (0,)), ((), ())),
        precision=lax.Precision.HIGHEST,
        preferred_element_type=jnp.float32,
    )


def ring_order(n_rows):
    return list(range(0, n_rows, 2)) + list(range(n_rows - 1, 0, -2))


def flip(n, bit):
    return [(i, i ^ bit) for i in range(n)]


def sum_cols(value, col_id):
    half = value.shape[0] // 2
    low, high_rows = value[:half], value[half:]
    first = col_id == 0
    sent = jnp.where(first, high_rows, low)
    return jnp.where(first, low, high_rows) + lax.ppermute(sent, "col", SWAP)


def fold_cols(value, col_id, n_rows):
    block, width = value.shape[0] // n_rows, value.shape[1]
    value = value.reshape(n_rows, 2, block // 2, width)
    first = col_id == 0
    sent = jnp.where(first, value[:, 1], value[:, 0])
    return jnp.where(first, value[:, 0], value[:, 1]) + lax.ppermute(sent, "col", SWAP)


def scatter_step(value, row_id, n_rows, bit):
    pairs = value.reshape(-1, 2, *value.shape[1:])
    zero = (row_id & bit) == 0
    kept = jnp.where(zero, pairs[:, 0], pairs[:, 1])
    sent = jnp.where(zero, pairs[:, 1], pairs[:, 0])
    return kept + lax.ppermute(sent, "row", flip(n_rows, bit))


def scatter_rows(value, row_id, n_rows):
    bit = 1
    while bit < n_rows:
        value = scatter_step(value, row_id, n_rows, bit)
        bit *= 2
    return value[0]


def split(value):
    coarse = value.astype(jnp.bfloat16)
    return coarse, (value - coarse.astype(jnp.float32)).astype(jnp.bfloat16)


def product(left, right, contract):
    dims = (((contract[0],), (contract[1],)), ((), ()))

    def dot(a, b):
        return lax.dot_general(a, b, dims, preferred_element_type=jnp.float32)

    coarse, fine = split(left)
    if right.dtype == jnp.bfloat16:
        return dot(coarse, right) + dot(fine, right)
    right_coarse, right_fine = split(right)
    return dot(coarse, right_coarse) + (dot(coarse, right_fine) + dot(fine, right_coarse))


def piece_kernel(count, has_total, places, *refs):
    blocks, pieces = refs[:count], refs[count : 2 * count]
    total, out = refs[2 * count], refs[-1]
    acc = total[...] if has_total else None
    for block, piece in zip(blocks, pieces):
        for part in split(block[...]):
            term = jnp.dot(part, piece[...], preferred_element_type=jnp.float32)
            acc = term if acc is None else acc + term
    out[...] = acc


def add_pieces(total, matrix, pieces, places):
    rows, width = matrix.shape[0], pieces[0][0].shape[1]
    tile = 512 if rows % 512 == 0 else 256

    def columns(depth, index):
        return pl.BlockSpec((tile, depth), lambda i, where: (i, where[index]))

    def part(depth, block):
        return pl.BlockSpec((depth, width), lambda i, where: (block, 0))

    specs = [columns(depth, index) for _, _, depth, index in pieces]
    specs += [part(depth, block) for _, block, depth, _ in pieces]
    args = [matrix] * len(pieces) + [array for array, _, _, _ in pieces]
    line = pl.BlockSpec((tile, width), lambda i, where: (i, 0))
    aliases = {}
    if total is not None:
        aliases = {1 + len(args): 0}
        specs.append(line)
        args.append(total)
    depth = sum(p[2] for p in pieces)
    return pl.pallas_call(
        lambda *refs: piece_kernel(len(pieces), total is not None, *refs),
        out_shape=jax.ShapeDtypeStruct((rows, width), jnp.float32),
        grid_spec=pltpu.PrefetchScalarGridSpec(
            num_scalar_prefetch=1, grid=(rows // tile,), in_specs=specs, out_specs=line
        ),
        input_output_aliases=aliases,
        compiler_params=pltpu.CompilerParams(vmem_limit_bytes=40 * 1024 * 1024),
        cost_estimate=pl.CostEstimate(
            flops=8 * rows * depth * width, bytes_accessed=4 * rows * depth, transcendentals=0
        ),
    )(places, *args)


def late_kernel(grad, late, early, top, inv_late, inv_early, late_cot, both):
    width = late_cot.shape[1]
    cot = -2.0 * product(grad[...], inv_late[...], (1, 1))
    late_cot[...] = cot
    late_term = -product(cot, late[...], (0, 0))
    corner = product(cot, early[...], (0, 0))
    corner += product(0.5 * (late_term + late_term.T), top[...], (1, 0))
    both[:, :width] = late_term
    both[:, width:] = -2.0 * product(corner, inv_early[...], (1, 1))


def late_chain(grad, late, early, top, inv_late, inv_early):
    rows, width = grad.shape
    return pl.pallas_call(
        late_kernel,
        out_shape=(
            jax.ShapeDtypeStruct((rows, width), jnp.float32),
            jax.ShapeDtypeStruct((width, 2 * width), jnp.float32),
        ),
        compiler_params=pltpu.CompilerParams(vmem_limit_bytes=40 * 1024 * 1024),
        cost_estimate=pl.CostEstimate(
            flops=16 * rows * width * width, bytes_accessed=8 * rows * width, transcendentals=0
        ),
    )(grad, late, early, top, inv_late, inv_early)


def early_kernel(grad, early, share, inv_early, early_cot, early_term):
    cot = -2.0 * product(grad[...], inv_early[...], (1, 1))
    early_cot[...] = cot
    early_term[...] = share[...] - product(cot, early[...], (0, 0))


def early_chain(grad, early, share, inv_early):
    rows, width = grad.shape
    return pl.pallas_call(
        early_kernel,
        out_shape=(
            jax.ShapeDtypeStruct((rows, width), jnp.float32),
            jax.ShapeDtypeStruct((width, width), jnp.float32),
        ),
        compiler_params=pltpu.CompilerParams(vmem_limit_bytes=40 * 1024 * 1024),
        cost_estimate=pl.CostEstimate(
            flops=10 * rows * width * width, bytes_accessed=8 * rows * width, transcendentals=0
        ),
    )(grad, early, share, inv_early)


def ring_places(n_rows, row_id):
    order = ring_order(n_rows)
    where = [0] * n_rows
    for place, row in enumerate(order):
        where[row] = place
    entries = [(0, 1, 0)]
    for step in range(1, n_rows // 2):
        entries += [(-step, 1, 0), (step, 1, 0)]
    half_at = {}
    for step in range(1, n_rows // 2 + 1):
        for way, sign in ((0, -1), (1, 1)):
            for half in (0, 1):
                half_at[way, step, half] = len(entries)
                entries.append((sign * step, 2, half))
    offset, scale, shift = (jnp.array(part, jnp.int32) for part in zip(*entries))
    place = jnp.array(where, jnp.int32)[row_id]
    owner = jnp.array(order, jnp.int32)[(place + offset + n_rows) % n_rows]
    return owner, owner * scale + shift, half_at


def by_ring(cot, late_masked, panel_early, inv_late, inv_early, trailing, own_start):
    n_rows = lax.axis_size("row")
    row_id = lax.axis_index("row")
    col_id = lax.axis_index("col")
    piece_rows, width = late_masked.shape
    first = col_id == 0
    is_root = (row_id == 0) & first
    owner, places, half_at = ring_places(n_rows, row_id)
    half = piece_rows // 2
    mid = n_rows // 2
    local = jnp.arange(piece_rows, dtype=jnp.int32)[:, None]
    order = ring_order(n_rows)
    ahead = [(order[i], order[(i + 1) % n_rows]) for i in range(n_rows)]
    ways = (ahead, [(b, a) for a, b in ahead])
    tie = lax.optimization_barrier

    def lead(value, way):
        return value[:half] if way == 0 else value[half:]

    def rest(value, way):
        return value[half:] if way == 0 else value[:half]

    def send(held):
        return list(tie(tuple(lax.ppermute(h, "row", way) for h, way in zip(held, ways))))

    def kept(piece, index, start):
        zero = first & (owner[index] == 0) & (local[start : start + piece.shape[0]] < width)
        return jnp.where(zero, jnp.zeros_like(piece), piece)

    sent = jnp.where(is_root & (local < width), panel_early, late_masked)
    late_part = add_pieces(None, cot, [(late_masked, 0, piece_rows, 0)], places)
    early_part = add_pieces(None, cot, [(panel_early, 0, piece_rows, 0)], places)
    top = jnp.where(is_root, sent[:width], jnp.zeros_like(sent[:width]))
    held = [sent, sent]
    for step in range(1, mid):
        held = send(held)
        if step == 1:
            late_part, *held = tie((late_part, *held))
        else:
            late_part, early_part, *held = tie((late_part, early_part, *held))
        pieces = []
        for way, piece in enumerate(held):
            index = 2 * step - 1 + way
            top = jnp.where(first & (owner[index] == 0), piece[:width], top)
            pieces.append((kept(piece, index, 0), 0, piece_rows, index))
        late_part = add_pieces(late_part, cot, pieces, places)

    held = [jnp.concatenate([lead(h, w), lead(panel_early, w)]) for w, h in enumerate(held)]
    held = send(held)
    late_part, *held = tie((late_part, *held))
    far = [half_at[0, mid, 0], half_at[1, mid, 1]]
    whole = jnp.concatenate([h[:half] for h in held])
    top = jnp.where(first & (owner[far[0]] == 0), whole[:width], top)
    pieces = [(kept(h[:half], far[w], w * half), 0, half, far[w]) for w, h in enumerate(held)]
    late_part = add_pieces(late_part, cot, pieces, places)
    waiting = [(h, 1, half, half_at[w, 1, w]) for w, h in enumerate(held)]

    for step in range(1, mid):
        if step == 1:
            held = [jnp.concatenate([rest(panel_early, w), h[half:]]) for w, h in enumerate(held)]
        held = send(held)
        if step == 1:
            top = jnp.where(first, top, lax.ppermute(top, "col", [(0, 1)]))
            late_grad = jnp.where(trailing, sum_cols(late_part, col_id), jnp.float32(0.0))
            late_grad, top, *held = tie((late_grad, top, *held))
            late_cot, both = late_chain(late_grad, late_masked, panel_early, top, inv_late, inv_early)
            corner_cot = both[:, width:]
        elif step == 2:
            early_part, both, *held = tie((early_part, both, *held))
            both = fold_cols(both, col_id, n_rows)
        else:
            early_part, *held = tie((early_part, *held))
        for w, h in enumerate(held):
            waiting.append((h, 0, half, half_at[w, step, 1 - w]))
            waiting.append((h, 1, half, half_at[w, step + 1, w]))
        early_part = add_pieces(early_part, cot, waiting, places)
        waiting = []

    both = scatter_rows(both, row_id, n_rows)
    top_f = top.astype(jnp.float32)
    extra = high(late_cot, top_f)
    corner_share = -high(corner_cot, top_f, (0, 0))
    early_grad = sum_cols(early_part, col_id) + extra
    early_cot, early_term = early_chain(early_grad, panel_early, corner_share, inv_early)
    early_own = scatter_rows(fold_cols(early_term, col_id, n_rows), row_id, n_rows)
    own = both[:, width:]
    blocks = [own] + [lax.ppermute(own, "row", [(k, 0)]) for k in range(1, n_rows)]
    mine = jnp.stack([both[:, :width], early_own] + blocks)
    other = lax.ppermute(mine, "col", SWAP)
    joined = jnp.stack([jnp.where(first, mine, other), jnp.where(first, other, mine)], axis=1)
    joined = joined.reshape(n_rows + 2, -1, width)
    corner = jnp.where(is_root, joined[2:].reshape(width, width), jnp.float32(0.0))
    early_cot = jnp.concatenate([early_cot[:width] + corner, early_cot[width:]], axis=0)
    return (late_cot, early_cot, joined[0], joined[1])


def by_gather(cot, late_masked, panel_early, inv_late, inv_early, trailing, own_start):
    piece_rows, panel_width = late_masked.shape
    strip_rows = cot.shape[0]
    early_f = panel_early.astype(jnp.float32)
    col_id = lax.axis_index("col")
    late_all = lax.all_gather(late_masked, "row", axis=0, tiled=True)
    late_part = highest(cot, late_all.astype(jnp.float32))
    early_all = lax.all_gather(panel_early, "row", axis=0, tiled=True)
    early_part = highest(cot, early_all.astype(jnp.float32))
    strips = -(-panel_width // strip_rows)
    own_top = early_all[: strips * piece_rows].reshape(strips, piece_rows, panel_width)
    top_block = lax.all_gather(own_top, "col", axis=1).reshape(-1, panel_width)[:panel_width]
    top_block = top_block.astype(jnp.float32)
    late_grad = jnp.where(trailing, sum_cols(late_part, col_id), jnp.float32(0.0))
    late_cot = -2.0 * highest(late_grad, inv_late.T)
    late_term = -inner_rows(late_cot, late_masked.astype(jnp.float32))
    cross_term = inner_rows(late_cot, early_f)
    corner_term = cross_term + highest(0.5 * (late_term + late_term.T), top_block)
    corner = lax.psum(corner_term, ("row", "col"))
    corner_padded = jnp.concatenate(
        [corner, jnp.zeros((piece_rows, panel_width), jnp.float32)], axis=0
    )
    corner_rows = lax.dynamic_slice_in_dim(
        corner_padded, jnp.minimum(own_start, panel_width), piece_rows, 0
    )
    extra = highest(late_cot, top_block) + corner_rows
    early_grad = sum_cols(early_part, col_id) + extra
    early_cot = -2.0 * highest(early_grad, inv_early.T)
    early_term = -inner_rows(early_cot, early_f)
    late_diag, early_diag = (
        lax.psum(lax.psum_scatter(term, "row", scatter_dimension=0, tiled=True), "col")
        for term in (late_term, early_term)
    )
    return (late_cot, early_cot, late_diag, early_diag)


def per_device(cot, panel_late, panel_early, inv_late, inv_early):
    strip_rows = cot.shape[0]
    piece_rows, panel_width = panel_late.shape
    n_rows = lax.axis_size("row")
    own_start = lax.axis_index("row") * strip_rows + lax.axis_index("col") * piece_rows
    positions = own_start + jnp.arange(piece_rows, dtype=jnp.int32)
    trailing = (positions >= panel_width)[:, None]
    late_masked = jnp.where(trailing, panel_late, jnp.zeros_like(panel_late))
    few = n_rows <= 16 and n_rows & (n_rows - 1) == 0 and piece_rows >= panel_width
    plan = by_ring if few and piece_rows % 256 == 0 else by_gather
    return plan(cot, late_masked, panel_early, inv_late, inv_early, trailing, own_start)


def solution(mesh):
    return jax.shard_map(
        per_device,
        mesh=mesh,
        in_specs=(
            P(("groups", "row"), "col"),
            P(("groups", "row", "col"), None),
            P(("groups", "row", "col"), None),
            P("groups", None),
            P("groups", None),
        ),
        out_specs=(
            P(("groups", "row", "col"), None),
            P(("groups", "row", "col"), None),
            P(("groups", "row"), None),
            P(("groups", "row"), None),
        ),
        check_vma=False,
    )
```

```python
import jax
import jax.numpy as jnp
from jax import lax
from jax.experimental import pallas as pl
from jax.experimental.pallas import tpu as pltpu
from jax.sharding import PartitionSpec as P

SWAP = [(0, 1), (1, 0)]


def high(left, right, contract=(1, 0)):
    return lax.dot_general(
        left,
        right,
        (((contract[0],), (contract[1],)), ((), ())),
        precision=lax.Precision.HIGH,
        preferred_element_type=jnp.float32,
    )


def highest(left, right):
    return jnp.dot(left, right, precision=lax.Precision.HIGHEST, preferred_element_type=jnp.float32)


def inner_rows(left, right):
    return lax.dot_general(
        left,
        right,
        (((0,), (0,)), ((), ())),
        precision=lax.Precision.HIGHEST,
        preferred_element_type=jnp.float32,
    )


def ring_order(n_rows):
    return list(range(0, n_rows, 2)) + list(range(n_rows - 1, 0, -2))


def flip(n, bit):
    return [(i, i ^ bit) for i in range(n)]


def sum_cols(value, col_id):
    half = value.shape[0] // 2
    low, high_rows = value[:half], value[half:]
    first = col_id == 0
    sent = jnp.where(first, high_rows, low)
    return jnp.where(first, low, high_rows) + lax.ppermute(sent, "col", SWAP)


def fold_cols(value, col_id, n_rows):
    block, width = value.shape[0] // n_rows, value.shape[1]
    value = value.reshape(n_rows, 2, block // 2, width)
    first = col_id == 0
    sent = jnp.where(first, value[:, 1], value[:, 0])
    return jnp.where(first, value[:, 0], value[:, 1]) + lax.ppermute(sent, "col", SWAP)


def scatter_step(value, row_id, n_rows, bit):
    pairs = value.reshape(-1, 2, *value.shape[1:])
    zero = (row_id & bit) == 0
    kept = jnp.where(zero, pairs[:, 0], pairs[:, 1])
    sent = jnp.where(zero, pairs[:, 1], pairs[:, 0])
    return kept + lax.ppermute(sent, "row", flip(n_rows, bit))


def scatter_rows(value, row_id, n_rows):
    bit = 1
    while bit < n_rows:
        value = scatter_step(value, row_id, n_rows, bit)
        bit *= 2
    return value[0]


def join_cols(value, col_id):
    other = lax.ppermute(value, "col", SWAP)
    first = col_id == 0
    return jnp.concatenate([jnp.where(first, value, other), jnp.where(first, other, value)], axis=0)


def gather_blocks(value, row_id, col_id, n_rows):
    half, width = value.shape
    value = value[None]
    bit = n_rows // 2
    while bit:
        other = lax.ppermute(value, "row", flip(n_rows, bit))
        zero = (row_id & bit) == 0
        value = jnp.stack([jnp.where(zero, value, other), jnp.where(zero, other, value)], axis=1)
        value = value.reshape(-1, half, width)
        bit //= 2
    other = lax.ppermute(value, "col", SWAP)
    first = col_id == 0
    both = jnp.stack([jnp.where(first, value, other), jnp.where(first, other, value)], axis=1)
    return both.reshape(-1, width)


def split(value):
    coarse = value.astype(jnp.bfloat16)
    return coarse, (value - coarse.astype(jnp.float32)).astype(jnp.bfloat16)


def product(left, right, contract):
    dims = (((contract[0],), (contract[1],)), ((), ()))

    def dot(a, b):
        return lax.dot_general(a, b, dims, preferred_element_type=jnp.float32)

    coarse, fine = split(left)
    if right.dtype == jnp.bfloat16:
        return dot(coarse, right) + dot(fine, right)
    right_coarse, right_fine = split(right)
    return dot(coarse, right_coarse) + (dot(coarse, right_fine) + dot(fine, right_coarse))


def piece_kernel(count, has_total, places, *refs):
    blocks, pieces = refs[:count], refs[count : 2 * count]
    total, out = refs[2 * count], refs[-1]
    acc = total[...] if has_total else None
    for block, piece in zip(blocks, pieces):
        value = block[...]
        coarse = value.astype(jnp.bfloat16)
        fine = (value - coarse.astype(jnp.float32)).astype(jnp.bfloat16)
        for part in (coarse, fine):
            term = jnp.dot(part, piece[...], preferred_element_type=jnp.float32)
            acc = term if acc is None else acc + term
    out[...] = acc


def add_pieces(total, matrix, pieces, places, first_place):
    rows, width = matrix.shape[0], pieces[0].shape[1]
    tile = 512 if rows % 512 == 0 else 256
    count = len(pieces)

    def columns(which):
        return pl.BlockSpec((tile, pieces[which].shape[0]), lambda i, where: (i, where[first_place + which]))

    specs = [columns(k) for k in range(count)]
    specs += [pl.BlockSpec(p.shape, lambda i, where: (0, 0)) for p in pieces]
    args = [matrix] * count + list(pieces)
    line = pl.BlockSpec((tile, width), lambda i, where: (i, 0))
    aliases = {}
    if total is not None:
        aliases = {1 + len(args): 0}
        specs.append(line)
        args.append(total)
    depth = sum(p.shape[0] for p in pieces)
    return pl.pallas_call(
        lambda *refs: piece_kernel(count, total is not None, *refs),
        out_shape=jax.ShapeDtypeStruct((rows, width), jnp.float32),
        grid_spec=pltpu.PrefetchScalarGridSpec(
            num_scalar_prefetch=1, grid=(rows // tile,), in_specs=specs, out_specs=line
        ),
        input_output_aliases=aliases,
        compiler_params=pltpu.CompilerParams(vmem_limit_bytes=40 * 1024 * 1024),
        cost_estimate=pl.CostEstimate(
            flops=8 * rows * depth * width, bytes_accessed=4 * rows * depth, transcendentals=0
        ),
    )(places, *args)


def late_kernel(grad, late, early, top, inv_late, inv_early, late_cot, both):
    width = late_cot.shape[1]
    cot = -2.0 * product(grad[...], inv_late[...], (1, 1))
    late_cot[...] = cot
    late_term = -product(cot, late[...], (0, 0))
    corner = product(cot, early[...], (0, 0))
    corner += product(0.5 * (late_term + late_term.T), top[...], (1, 0))
    both[:, :width] = late_term
    both[:, width:] = -2.0 * product(corner, inv_early[...], (1, 1))


def late_chain(grad, late, early, top, inv_late, inv_early):
    rows, width = grad.shape
    return pl.pallas_call(
        late_kernel,
        out_shape=(
            jax.ShapeDtypeStruct((rows, width), jnp.float32),
            jax.ShapeDtypeStruct((width, 2 * width), jnp.float32),
        ),
        compiler_params=pltpu.CompilerParams(vmem_limit_bytes=40 * 1024 * 1024),
        cost_estimate=pl.CostEstimate(
            flops=16 * rows * width * width, bytes_accessed=8 * rows * width, transcendentals=0
        ),
    )(grad, late, early, top, inv_late, inv_early)


def early_kernel(grad, early, share, inv_early, early_cot, early_term):
    cot = -2.0 * product(grad[...], inv_early[...], (1, 1))
    early_cot[...] = cot
    early_term[...] = share[...] - product(cot, early[...], (0, 0))


def early_chain(grad, early, share, inv_early):
    rows, width = grad.shape
    return pl.pallas_call(
        early_kernel,
        out_shape=(
            jax.ShapeDtypeStruct((rows, width), jnp.float32),
            jax.ShapeDtypeStruct((width, width), jnp.float32),
        ),
        compiler_params=pltpu.CompilerParams(vmem_limit_bytes=40 * 1024 * 1024),
        cost_estimate=pl.CostEstimate(
            flops=10 * rows * width * width, bytes_accessed=8 * rows * width, transcendentals=0
        ),
    )(grad, early, share, inv_early)


class Ring:
    def __init__(self, piece, n_rows):
        order = ring_order(n_rows)
        self.ahead = [(order[i], order[(i + 1) % n_rows]) for i in range(n_rows)]
        self.back = [(b, a) for a, b in self.ahead]
        self.n, self.half = n_rows, piece.shape[0] // 2
        self.step = 0
        self.held = (piece, piece)

    def advance(self):
        self.step += 1
        before, after = self.held
        if self.step == self.n // 2:
            before, after = before[: self.half], after[self.half :]
        before = lax.ppermute(before, "row", self.ahead)
        after = lax.ppermute(after, "row", self.back)
        self.held = lax.optimization_barrier((before, after))
        return self.held


def ring_places(n_rows, row_id):
    order = ring_order(n_rows)
    where = [0] * n_rows
    for place, row in enumerate(order):
        where[row] = place
    offsets = [0]
    for step in range(1, n_rows // 2):
        offsets += [n_rows - step, step]
    offsets += [n_rows // 2] * 2
    place = jnp.array(where, jnp.int32)[row_id]
    whose = jnp.array(order, jnp.int32)[(place + jnp.array(offsets, jnp.int32)) % n_rows]
    scale = jnp.array([1] * (n_rows - 1) + [2, 2], jnp.int32)
    shift = jnp.array([0] * n_rows + [1], jnp.int32)
    return whose, whose * scale + shift


def by_ring(cot, late_masked, panel_early, inv_late, inv_early, trailing, own_start):
    n_rows = lax.axis_size("row")
    row_id = lax.axis_index("row")
    col_id = lax.axis_index("col")
    piece_rows, width = late_masked.shape
    first = col_id == 0
    is_root = (row_id == 0) & first
    whose, places = ring_places(n_rows, row_id)
    half = piece_rows // 2
    local = jnp.arange(piece_rows, dtype=jnp.int32)[:, None]

    sent = jnp.where(is_root & (local < width), panel_early, late_masked)

    def kept(piece, owner, start):
        lead = first & (owner == 0) & (local[start : start + piece.shape[0]] < width)
        return jnp.where(lead, jnp.zeros_like(piece), piece)

    ring = Ring(sent, n_rows)
    late_part = add_pieces(None, cot, [late_masked], places, 0)
    early_part = add_pieces(None, cot, [panel_early], places, 0)
    top = jnp.where(is_root, sent[:width], jnp.zeros_like(sent[:width]))
    for step in range(1, n_rows // 2):
        came = ring.advance()
        if step == 1:
            late_part, *came = lax.optimization_barrier((late_part, *came))
        if step == 2:
            early_part, *came = lax.optimization_barrier((early_part, *came))
        ring.held = came
        at = 2 * step - 1
        for which, piece in enumerate(came):
            top = jnp.where(first & (whose[at + which] == 0), piece[:width], top)
        pieces = [kept(piece, whose[at + which], 0) for which, piece in enumerate(came)]
        late_part = add_pieces(late_part, cot, pieces, places, at)
    panel_next, *ring.held = lax.optimization_barrier((panel_early, *ring.held))
    low, high_rows = ring.advance()
    far = whose[n_rows - 1]
    top = jnp.where(first & (far == 0), jnp.concatenate([low, high_rows], axis=0)[:width], top)
    pieces = [kept(low, far, 0), kept(high_rows, far, half)]
    late_part = add_pieces(late_part, cot, pieces, places, n_rows - 1)

    ring = Ring(panel_next, n_rows)
    top = jnp.where(first, top, lax.ppermute(top, "col", [(0, 1)]))
    late_grad = jnp.where(trailing, sum_cols(late_part, col_id), jnp.float32(0.0))
    late_cot, both = late_chain(late_grad, late_masked, panel_early, top, inv_late, inv_early)
    corner_cot = both[:, width:]
    top_f = top.astype(jnp.float32)
    extra = high(late_cot, top_f)
    corner_share = -high(corner_cot, top_f, (0, 0))
    both = fold_cols(both, col_id, n_rows)
    bit = 1
    for step in range(1, n_rows // 2 + 1):
        came = ring.advance()
        if step > 1:
            early_part, *came = lax.optimization_barrier((early_part, *came))
        if step > 2 and bit < n_rows:
            both = scatter_step(both, row_id, n_rows, bit)
            bit *= 2
            both, *came = lax.optimization_barrier((both, *came))
        ring.held = came
        early_part = add_pieces(early_part, cot, came, places, 2 * step - 1)
    while bit < n_rows:
        both = scatter_step(both, row_id, n_rows, bit)
        bit *= 2
    both = both[0]
    late_diag = join_cols(both[:, :width], col_id)
    corner = gather_blocks(both[:, width:], row_id, col_id, n_rows)

    early_grad = sum_cols(early_part, col_id) + extra
    early_cot, early_term = early_chain(early_grad, panel_early, corner_share, inv_early)
    early_diag = join_cols(
        scatter_rows(fold_cols(early_term, col_id, n_rows), row_id, n_rows), col_id
    )
    top_rows = early_cot[:width] + jnp.where(is_root, corner, jnp.float32(0.0))
    early_cot = jnp.concatenate([top_rows, early_cot[width:]], axis=0)
    return (late_cot, early_cot, late_diag, early_diag)


def by_gather(cot, late_masked, panel_early, inv_late, inv_early, trailing, own_start):
    piece_rows, panel_width = late_masked.shape
    strip_rows = cot.shape[0]
    early_f = panel_early.astype(jnp.float32)
    col_id = lax.axis_index("col")
    late_all = lax.all_gather(late_masked, "row", axis=0, tiled=True)
    late_part = highest(cot, late_all.astype(jnp.float32))
    early_all = lax.all_gather(panel_early, "row", axis=0, tiled=True)
    early_part = highest(cot, early_all.astype(jnp.float32))
    strips = -(-panel_width // strip_rows)
    own_top = early_all[: strips * piece_rows].reshape(strips, piece_rows, panel_width)
    top_block = lax.all_gather(own_top, "col", axis=1).reshape(-1, panel_width)[:panel_width]
    top_block = top_block.astype(jnp.float32)
    late_grad = jnp.where(trailing, sum_cols(late_part, col_id), jnp.float32(0.0))
    late_cot = -2.0 * highest(late_grad, inv_late.T)
    late_term = -inner_rows(late_cot, late_masked.astype(jnp.float32))
    cross_term = inner_rows(late_cot, early_f)
    corner_term = cross_term + highest(0.5 * (late_term + late_term.T), top_block)
    corner = lax.psum(corner_term, ("row", "col"))
    corner_padded = jnp.concatenate(
        [corner, jnp.zeros((piece_rows, panel_width), jnp.float32)], axis=0
    )
    corner_rows = lax.dynamic_slice_in_dim(
        corner_padded, jnp.minimum(own_start, panel_width), piece_rows, 0
    )
    extra = highest(late_cot, top_block) + corner_rows
    early_grad = sum_cols(early_part, col_id) + extra
    early_cot = -2.0 * highest(early_grad, inv_early.T)
    early_term = -inner_rows(early_cot, early_f)
    late_diag, early_diag = (
        lax.psum(lax.psum_scatter(term, "row", scatter_dimension=0, tiled=True), "col")
        for term in (late_term, early_term)
    )
    return (late_cot, early_cot, late_diag, early_diag)


def per_device(cot, panel_late, panel_early, inv_late, inv_early):
    strip_rows = cot.shape[0]
    piece_rows, panel_width = panel_late.shape
    n_rows = lax.axis_size("row")
    own_start = lax.axis_index("row") * strip_rows + lax.axis_index("col") * piece_rows
    positions = own_start + jnp.arange(piece_rows, dtype=jnp.int32)
    trailing = (positions >= panel_width)[:, None]
    late_masked = jnp.where(trailing, panel_late, jnp.zeros_like(panel_late))
    few = n_rows <= 16 and n_rows & (n_rows - 1) == 0 and piece_rows >= panel_width
    plan = by_ring if few and piece_rows % 256 == 0 else by_gather
    return plan(cot, late_masked, panel_early, inv_late, inv_early, trailing, own_start)


def solution(mesh):
    return jax.shard_map(
        per_device,
        mesh=mesh,
        in_specs=(
            P(("groups", "row"), "col"),
            P(("groups", "row", "col"), None),
            P(("groups", "row", "col"), None),
            P("groups", None),
            P("groups", None),
        ),
        out_specs=(
            P(("groups", "row", "col"), None),
            P(("groups", "row", "col"), None),
            P(("groups", "row"), None),
            P(("groups", "row"), None),
        ),
        check_vma=False,
    )
```
